256 devices in a mesh: band: 16 (over y_hi, z), comp: 16 (over y_lo, x, core).
Axes of the slice: x: 4, y: 4 (y_hi: 2, y_lo: 2; y = y_hi * 2 + y_lo), z: 8, core: 2. Of those that a mesh axis runs over, the one named last changes fastest.
Arguments:
- pair_dens: bfloat16 [6144, 8192], P('band', 'comp'), may hold values from -0.29882812 to 0.29882812
- pair_index: int32 [6144], P('band'), may hold values from 0 to 6143, each once
- val_energy: float32 [24], replicated, may hold values from -9 to -1
- cond_energy: float32 [256], replicated, may hold values from 0.5 to 12
- coul_root: float32 [8192], replicated, may hold values from 0.5 to 2
Outputs:
- epsilon: float32 [8192, 8192], P('band', 'comp')
- panel_factor: float32 [8192, 128], P(('band', 'comp'))
The draws below stay inside these ranges and needn't reach their ends.
Inputs may be any that keep to these rules, and one draw needn't show every extreme that they name: `pair_index`: every pair number appears exactly once; pair number n joins valence band n // 256 with conduction band n % 256.
All inputs are finite; a program needn't handle non-finite values.
Results may differ from the reference program's by a relative error of at most 0.0022.
Values may be sent and summed in bfloat16 or wider, within the bound.
A program may use at most 64 MiB of HBM per device.

```python
import math
import jax
import jax.numpy as jnp
from jax import lax

VAL = 24
COND = 256
PAIRS = 6144
G = 8192
PANEL = 128


def steps_of(rng, shape, split, least, high):
    level = 1.0
    for dim, parts in split:
        steps = jax.random.uniform(jax.random.fold_in(jax.random.fold_in(rng, 6), dim), (parts,), jnp.float32, least / len(split), high / len(split))
        level = level * jnp.repeat(jnp.exp(steps), shape[dim] // parts).reshape((-1,) + (1,) * (len(shape) - 1 - dim))
    return level


def scatter_about(key, extent, deviation, most, shards=(), kind=jnp.bfloat16):
    result = deviation * jax.random.normal(key, extent, jnp.float32)
    if shards:
        result = result * steps_of(key, extent, shards, -0.22, 0.18)
    return jnp.clip(result, -most, most).astype(kind)


def setup_inputs(seed: int = 0) -> dict:
    arg_keys = jax.random.split(jax.random.key(seed), 6)
    pair_dens = scatter_about(arg_keys[0], (PAIRS, G), 0.05, 0.29882812, ((0, 16), (1, 16)))
    pair_index = jax.random.permutation(arg_keys[1], PAIRS).astype(jnp.int32)
    val_energy = jnp.clip(jax.random.uniform(arg_keys[2], (VAL,), jnp.float32, -9.0, -1.0), -9.0, -1.0)
    cond_energy = jnp.clip(jax.random.uniform(arg_keys[3], (COND,), jnp.float32, 0.5, 12.0), 0.5, 12.0)
    coul_root = jnp.clip(jnp.exp(jax.random.uniform(arg_keys[4], (G,), jnp.float32, math.log(0.5), math.log(2.0))), 0.5, 2.0)
    return {"pair_dens": pair_dens, "pair_index": pair_index, "val_energy": val_energy, "cond_energy": cond_energy, "coul_root": coul_root}


def reference(pair_dens, pair_index, val_energy, cond_energy, coul_root):
    valence = pair_index // COND
    conduction = pair_index % COND
    weight = 4.0 / (cond_energy[conduction] - val_energy[valence])
    dens_wide = pair_dens.astype(jnp.float32)
    scaled = (weight[:, None] * dens_wide).astype(jnp.bfloat16)
    chi = jnp.dot(dens_wide.T, scaled.astype(jnp.float32), precision=lax.Precision.HIGHEST)
    epsilon = coul_root[:, None] * chi * coul_root[None, :] + jnp.eye(G, dtype=jnp.float32)
    top = jnp.linalg.cholesky(epsilon[:PANEL, :PANEL])
    panel_factor = jax.scipy.linalg.solve_triangular(top, epsilon[:, :PANEL].T, lower=True).T
    return (epsilon, panel_factor)
```

```python
import functools

import jax
import jax.numpy as jnp
from jax import lax
from jax.experimental import pallas as pl
from jax.experimental.pallas import tpu as pltpu
from jax.sharding import PartitionSpec as P

VAL = 24
COND = 256
PANEL = 128
MESH = pl.DeviceIdType.MESH

ROWS = 384
WIDTH = 512
NZ = 8
NC = 4
HS = WIDTH // NC
NP = WIDTH // PANEL
EARLY = 4
STEPS = 5
BLOCK = 16
ORDER = ((0, 0), (1, 0), (0, 1), (2, 0), (0, 2), (1, 1), (3, 0), (0, 3), (1, 2), (0, 4),
         (2, 1), (1, 3), (3, 1), (2, 2), (1, 4), (3, 2), (2, 3), (3, 3), (2, 4), (3, 4))
SUMS = ((0, 0), (1, 0), (0, 1), (2, 0), (3, 0), (0, 2), (1, 1), (0, 3), (1, 2), (0, 4),
        (1, 3), (1, 4), (2, 1), (3, 1), (2, 2), (3, 2), (2, 3), (3, 3), (2, 4), (3, 4))
LAG = 15
START = 12
RING = 2


def device(yl, x, k, yh, z):
    return (yh * NZ + z, yl * 8 + x * 2 + k)


def crossed(d):
    return jnp.logical_and(d >= 1, d <= 4)


def kernel(dens_in, index_in, val_in, cond_in, root_in, out, panel,
           dens, index, val_energy, cond_energy, root, in_sem, it, st, w, acc, sendb, recvb, outb, half, other, both_sides, prows, pmine,
           j_send, j_recv, w_send, w_recv, i_recv, x_send, y_send, s_send,
           p_send, p_recv, o_sem, a_sem, f_send, f_recv):
    b = lax.axis_index("band")
    c = lax.axis_index("comp")
    yh, z = b // NZ, b % NZ
    yl, x, k = c // 8, (c // 2) % 4, c % 2
    x0, k0 = z // 2, z % 2
    xr = (x - x0 + 4) % 4
    source_chip = xr == 0
    source = jnp.logical_and(source_chip, k == k0)

    up = device(yl, x, k, yh, (z + 1) % NZ)
    down = device(yl, x, k, yh, (z + NZ - 1) % NZ)
    xp = (x + 1) % 4
    xm = (x + 3) % 4
    sibling = device(yl, x, 1 - k, yh, z)
    far = device(yl, x, k, 1 - yh, z)

    load_dens = pltpu.make_async_copy(dens_in, dens, in_sem.at[0])
    load_root = pltpu.make_async_copy(root_in, root, in_sem.at[1])
    loads = (pltpu.make_async_copy(index_in, index, in_sem.at[2]),
             pltpu.make_async_copy(val_in, val_energy, in_sem.at[3]),
             pltpu.make_async_copy(cond_in, cond_energy, in_sem.at[4]),
             load_root)
    load_dens.start()
    for load in loads:
        load.start()
    barrier = pltpu.get_barrier_semaphore()
    partners = [up, down, sibling, far]
    for core in (0, 1):
        partners.append(device(yl, xp, core, yh, z))
        partners.append(device(yl, xm, core, yh, z))
        partners.append(device(1 - yl, x, core, yh, z))
    for partner in partners:
        pl.semaphore_signal(barrier, inc=1, device_id=partner, device_id_type=MESH)

    load_dens.wait()
    for n in range(NC):
        it[RING, 0, n] = dens[:, n * HS:(n + 1) * HS].T

    lead = c == 0

    def column(i):
        return (b, i)

    @pl.when(lead)
    def _():
        for i in range(1, 16):
            pl.semaphore_signal(barrier, inc=1, device_id=column(i), device_id_type=MESH)

    @pl.when(c != 0)
    def _():
        pl.semaphore_signal(barrier, inc=1, device_id=column(0), device_id_type=MESH)

    pl.semaphore_wait(barrier, len(partners) + jnp.where(lead, 15, 1))

    def j_copy(n, d, target):
        later = d + 1 if target is down else (d + NZ - 1) % NZ
        return pltpu.make_async_remote_copy(
            it.at[RING, d, n], it.at[RING, later, n], j_send.at[n, later], j_recv.at[n, later],
            device_id=target, device_id_type=MESH)

    def j_wait(n, d):
        pltpu.make_async_remote_copy(
            it.at[RING, d, n], it.at[RING, d, n], j_send.at[n, d], j_recv.at[n, d],
            device_id=up, device_id_type=MESH).wait_recv()

    def w_copy(d, target):
        later = d + 1 if target is down else (d + NZ - 1) % NZ
        return pltpu.make_async_remote_copy(
            w.at[d], w.at[later], w_send.at[later], w_recv.at[later],
            device_id=target, device_id_type=MESH)

    def w_wait(d):
        pltpu.make_async_remote_copy(
            w.at[d], w.at[d], w_send.at[d], w_recv.at[d],
            device_id=up, device_id_type=MESH).wait_recv()

    def own_sends(n):
        j_copy(n, 0, down).start()
        j_copy(n, 0, up).start()

    def i_copy(src, blk, n, d, send, target):
        return pltpu.make_async_remote_copy(
            src, it.at[blk, d, n], send, i_recv.at[blk, n, d],
            device_id=target, device_id_type=MESH)

    def i_wait(blk, n, d):
        i_copy(it.at[blk, d, n], blk, n, d, s_send.at[blk, n, d], sibling).wait_recv()

    def source_copies(n, d):
        src = it.at[RING, d, n]
        h = n % 2
        return [
            i_copy(src, yl, n, d, y_send.at[n, d], device(1 - yl, x, h, yh, z)),
            i_copy(src, yl, n, d, x_send.at[yl, n, d], device(yl, (x + 5 - 2 * h) % 4, h, yh, z)),
            i_copy(src, yl, n, d, s_send.at[yl, n, d], sibling),
        ]

    def source_sends(n, d):
        for copy in source_copies(n, d):
            copy.start()

    own_sends(0)
    own_sends(1)

    for load in loads:
        load.wait()
    number = jnp.broadcast_to(index[...].reshape(1, ROWS), (8, ROWS))
    valence = number // COND
    conduction = number % COND

    def pick(table, which, n):
        def body(i, kept):
            return jnp.where(which == i, table[i], kept)
        return lax.fori_loop(0, n, body, jnp.zeros((8, ROWS), jnp.float32), unroll=8)

    high = pick(cond_energy, conduction, COND)
    low = pick(val_energy, valence, VAL)
    w[0] = 4.0 / (high - low)
    w_copy(0, down).start()
    w_copy(0, up).start()

    hops = jnp.where(k == 0, xr, (4 - xr) % 4)
    lag_x = hops * 3
    lag_y = lag_x + 3
    lag_c = LAG
    forward_x = jnp.where(k == 0, jnp.logical_or(xr == 1, xr == 2), jnp.logical_or(xr == 3, xr == 2))
    x_target = device(yl, (x + 5 - 2 * k) % 4, k, yh, z)
    y_target = device(1 - yl, x, k, yh, z)

    def x_copy(blk, n, d):
        return i_copy(it.at[blk, d, n], blk, n, d, x_send.at[blk, n, d], x_target)

    def y_copy(n, d):
        return i_copy(it.at[yl, d, n], yl, n, d, y_send.at[n, d], y_target)

    def s_copy(blk, n, d):
        return i_copy(it.at[blk, d, n], blk, n, d, s_send.at[blk, n, d], sibling)

    def j_step(n, t):
        h = n % 2
        inner = jnp.logical_and(t >= 1, t <= 3)

        @pl.when(inner)
        def _():
            j_wait(n, t)

            @pl.when(jnp.logical_or(t < 3, h == 0))
            def _():
                j_copy(n, t, down).start()
            j_wait(n, NZ - t)

            @pl.when(jnp.logical_or(t < 3, h == 1))
            def _():
                j_copy(n, NZ - t, up).start()

            @pl.when(n == 0)
            def _():
                w_wait(t)
                w_wait(NZ - t)
                w_copy(t, down).start()

                @pl.when(t < 3)
                def _():
                    w_copy(NZ - t, up).start()

        @pl.when(t == 4)
        def _():
            j_wait(n, 4)

            @pl.when(n == 0)
            def _():
                w_wait(4)

        @pl.when(source)
        def _():
            source_sends(n, t)

            @pl.when(inner)
            def _():
                source_sends(n, NZ - t)

    def both(act):
        def run(n, t):
            act(n, t)

            @pl.when(jnp.logical_and(t >= 1, t <= 3))
            def _():
                act(n, NZ - t)
        return run

    def x_step(n, d):
        @pl.when(jnp.logical_and(n % 2 == k, jnp.logical_not(source_chip)))
        def _():
            i_wait(yl, n, d)

            @pl.when(forward_x)
            def _():
                x_copy(yl, n, d).start()

            @pl.when(jnp.logical_not(crossed(d)))
            def _():
                y_copy(n, d).start()
            s_copy(yl, n, d).start()

    def y_step(n, d):
        @pl.when(n % 2 == k)
        def _():
            i_wait(1 - yl, n, d)

            @pl.when(jnp.logical_and(crossed(d), jnp.logical_or(source_chip, forward_x)))
            def _():
                x_copy(1 - yl, n, d).start()
            s_copy(1 - yl, n, d).start()

    own_row = jnp.where(source, RING, yl)

    def compute_step(n, t):
        def arrived(d):
            @pl.when(jnp.logical_not(source))
            def _():
                @pl.when(jnp.logical_or(source_chip, n % 2 != k))
                def _():
                    i_wait(yl, n, d)

            @pl.when(n % 2 != k)
            def _():
                i_wait(1 - yl, n, d)

        both(lambda n, d: arrived(d))(n, t)
        def rows(d):
            return jnp.concatenate([it[own_row, d, n], it[1 - yl, d, n]], axis=0)

        def product(left, right):
            return lax.dot_general(left, right, (((1,), (1,)), ((), ())), preferred_element_type=jnp.float32)

        @pl.when(t == 0)
        def _():
            part = product(rows(0), st[0])
            acc[yl, n] = part[:HS]
            acc[1 - yl, n] = part[HS:]

        @pl.when(jnp.logical_and(t >= 1, t <= 3))
        def _():
            part = product(jnp.concatenate([rows(t), rows(NZ - t)], axis=1),
                           jnp.concatenate([st[t], st[NZ - t]], axis=1))
            acc[yl, n] += part[:HS]
            acc[1 - yl, n] += part[HS:]

        @pl.when(t == 4)
        def _():
            part = product(rows(4), st[4])
            acc[yl, n] += part[:HS]
            acc[1 - yl, n] += part[HS:]
            for p in range(NP):
                sendb[n, p] = acc[1 - yh, n, :, p * PANEL:(p + 1) * PANEL].astype(jnp.bfloat16)
            for p in range(EARLY):
                p_copy(n, p).start()

            @pl.when(n == 0)
            def _():
                for p in range(EARLY, NP):
                    p_copy(0, p).start()

            @pl.when(n == NC - 1)
            def _():
                for p in range(EARLY, NP):
                    for i in range(1, NC):
                        p_copy(i, p).start()

    def scale(n, d):
        wide = it[RING, d, n].astype(jnp.float32)
        st[d, pl.ds(n * HS, HS)] = (w[d, 0:1, :] * wide).astype(jnp.bfloat16)

    def p_copy(n, p):
        return pltpu.make_async_remote_copy(
            sendb.at[n, p], recvb.at[n, p], p_send.at[n, p], p_recv.at[n, p],
            device_id=far, device_id_type=MESH)

    def o_copy(n, p):
        return pltpu.make_async_copy(
            outb.at[n, p], out.at[pl.ds(n * HS, HS), pl.ds(p * PANEL, PANEL)], o_sem.at[n, p])

    def finish(n, p):
        p_copy(n, p).wait_recv()
        row = root[pl.ds(b * 4 + n, 1), :]
        rows = jnp.broadcast_to(row, (128, 128)).T
        row_ids = b * WIDTH + n * HS + lax.broadcasted_iota(jnp.int32, (HS, 128), 0)
        col = root[pl.ds(c * 4 + p, 1), :]
        col_ids = c * WIDTH + p * PANEL + lax.broadcasted_iota(jnp.int32, (HS, PANEL), 1)
        unit = jnp.where(row_ids == col_ids, 1.0, 0.0).astype(jnp.float32)
        total = acc[yh, n, :, p * PANEL:(p + 1) * PANEL] + recvb[n, p].astype(jnp.float32)
        outb[n, p] = rows * total * col + unit
        o_copy(n, p).start()

    last = STEPS * NC

    def pick_event(e, order):
        code = 0
        for i in range(0, len(order), 6):
            word = sum((t * NC + n) << (5 * j) for j, (n, t) in enumerate(order[i:i + 6]))
            code = jnp.where(e >= i, (word >> (e % 6 * 5)) & 31, code)
        return code & 3, code >> 2

    def events(e, act):
        @pl.when(jnp.logical_and(e >= 0, e < last))
        def _():
            act(*pick_event(e, ORDER))

    def computes(e):
        @pl.when(jnp.logical_and(e >= 0, e < last))
        def _():
            compute_step(*pick_event(e, SUMS))

    def a_copy():
        return pltpu.make_async_remote_copy(
            half, other, a_sem.at[0], a_sem.at[1], device_id=far, device_id_type=MESH)

    def lead_part(d):
        half[...] += lax.dot_general(it[RING, d, 0], st[d, 0:HS], (((1,), (1,)), ((), ())),
                                     preferred_element_type=jnp.float32)

    def first(n, t):
        j_step(n, t)
        both(scale)(n, t)

        @pl.when(jnp.logical_and(t == 0, n + 2 < NC))
        def _():
            own_sends(n + 2)

        @pl.when(jnp.logical_and(lead, n == 0))
        def _():
            both(lambda n, d: lead_part(d))(n, t)

            @pl.when(t == 4)
            def _():
                a_copy().start()

    lanes = lax.broadcasted_iota(jnp.int32, (BLOCK, PANEL), 1)
    subs = lax.broadcasted_iota(jnp.int32, (BLOCK, 1), 0)

    def factor_begin():
        a_copy().wait_recv()
        row = root[0:1, :]
        rows = jnp.broadcast_to(row, (PANEL, PANEL)).T
        ids = lax.broadcasted_iota(jnp.int32, (PANEL, PANEL), 0)
        unit = jnp.where(ids == lax.broadcasted_iota(jnp.int32, (PANEL, PANEL), 1), 1.0, 0.0)
        block = rows * (half[...] + other[...]) * row + unit
        both_sides[:, 0:PANEL] = (block + block.T) * 0.5
        both_sides[:, PANEL:] = unit

    def factor_block(j):
        base = pl.multiple_of(j * BLOCK, BLOCK)
        rows = both_sides[pl.ds(base, BLOCK), :]
        for i in range(BLOCK):
            col = jnp.sum(jnp.where(lanes == base + i, rows[:, 0:PANEL], 0.0), axis=1, keepdims=True)
            pivot = col[i:i + 1]
            inv = lax.rsqrt(pivot)
            inv = inv * (1.5 - 0.5 * pivot * inv * inv)
            line = rows[i:i + 1] * inv
            rows = jnp.where(subs > i, rows - (col * inv) * line, jnp.where(subs == i, line, rows))
        below = jnp.where(lanes >= base + BLOCK, rows[:, 0:PANEL], 0.0)
        both_sides[pl.ds(base, BLOCK), :] = rows
        both_sides[...] -= lax.dot_general(below, rows, (((0,), (0,)), ((), ())),
                                           precision=lax.Precision.HIGHEST,
                                           preferred_element_type=jnp.float32)

    def turn(e, carry):
        events(e, first)
        events(e - lag_x, both(x_step))
        events(e - lag_y, both(y_step))
        computes(e - lag_c)

        @pl.when(lead)
        def _():
            @pl.when(e == START)
            def _():
                factor_begin()

            @pl.when(jnp.logical_and(e >= START, e < START + PANEL // BLOCK))
            def _():
                factor_block(e - START)
        return carry

    @pl.when(lead)
    def _():
        half[...] = jnp.zeros_like(half)

    lax.fori_loop(0, last + LAG, turn, 0)

    def sent(n, carry):
        def each(d, inner):
            @pl.when(source)
            def _():
                for copy in source_copies(n, d):
                    copy.wait_send()

            @pl.when(n % 2 == k)
            def _():
                @pl.when(jnp.logical_not(source_chip))
                def _():
                    @pl.when(forward_x)
                    def _():
                        x_copy(yl, n, d).wait_send()

                    @pl.when(jnp.logical_not(crossed(d)))
                    def _():
                        y_copy(n, d).wait_send()
                    s_copy(yl, n, d).wait_send()

                @pl.when(jnp.logical_and(crossed(d), jnp.logical_or(source_chip, forward_x)))
                def _():
                    x_copy(1 - yl, n, d).wait_send()
                s_copy(1 - yl, n, d).wait_send()
            return inner
        lax.fori_loop(0, NZ, each, 0)
        for d in range(1, NZ):
            if d < 4:
                j_copy(n, d - 1, down).wait_send()
            elif d > 4:
                j_copy(n, (d + 1) % NZ, up).wait_send()
            else:
                j_copy(n, 3, down).wait_send()
        return carry

    lax.fori_loop(0, NC, sent, 0)
    for d in range(1, NZ):
        if d <= 4:
            w_copy(d - 1, down).wait_send()
        else:
            w_copy((d + 1) % NZ, up).wait_send()

    def f_copy(i):
        return pltpu.make_async_remote_copy(
            prows.at[i], pmine, f_send.at[i], f_recv.at[0], device_id=column(i), device_id_type=MESH)

    def f_out(src):
        return pltpu.make_async_copy(src, panel, f_recv.at[1])

    for n in range(NC):
        finish(n, 0)

        @pl.when(lead)
        def _():
            solved = lax.dot_general(outb[n, 0], both_sides[:, PANEL:], (((1,), (1,)), ((), ())),
                                     precision=lax.Precision.HIGHEST, preferred_element_type=jnp.float32)
            for i in range(4):
                prows[4 * n + i] = solved[32 * i:32 * (i + 1)]
                if n or i:
                    f_copy(4 * n + i).start()
                else:
                    f_out(prows.at[0]).start()

    for p in range(1, NP):
        for n in range(NC):
            finish(n, p)

    @pl.when(c != 0)
    def _():
        f_copy(1).wait_recv()
        f_out(pmine).start()
        f_out(pmine).wait()

    @pl.when(lead)
    def _():
        f_out(prows.at[0]).wait()
        a_copy().wait_send()
        for i in range(1, 16):
            f_copy(i).wait_send()

    for n in range(NC):
        for p in range(NP):
            p_copy(n, p).wait_send()
            o_copy(n, p).wait()


def epsilon_block(pair_dens, pair_index, val_energy, cond_energy, coul_root):
    hbm = pl.BlockSpec(memory_space=pltpu.HBM)
    dma = pltpu.SemaphoreType.DMA
    return pl.pallas_call(
        kernel,
        out_shape=(jax.ShapeDtypeStruct((WIDTH, WIDTH), jnp.float32),
                   jax.ShapeDtypeStruct((WIDTH // 16, PANEL), jnp.float32)),
        in_specs=[hbm] * 5,
        out_specs=(pl.BlockSpec(memory_space=pl.ANY), pl.BlockSpec(memory_space=pl.ANY)),
        scratch_shapes=[
            pltpu.VMEM((ROWS, WIDTH), jnp.bfloat16),
            pltpu.VMEM((ROWS,), jnp.int32),
            pltpu.SMEM((VAL,), jnp.float32),
            pltpu.SMEM((COND,), jnp.float32),
            pltpu.VMEM((64, 128), jnp.float32),
            dma((5,)),
            pltpu.VMEM((3, NZ, NC, HS, ROWS), jnp.bfloat16),
            pltpu.VMEM((NZ, WIDTH, ROWS), jnp.bfloat16),
            pltpu.VMEM((NZ, 8, ROWS), jnp.float32),
            pltpu.VMEM((2, NC, HS, WIDTH), jnp.float32),
            pltpu.VMEM((NC, NP, HS, PANEL), jnp.bfloat16),
            pltpu.VMEM((NC, NP, HS, PANEL), jnp.bfloat16),
            pltpu.VMEM((NC, NP, HS, PANEL), jnp.float32),
            pltpu.VMEM((PANEL, PANEL), jnp.float32),
            pltpu.VMEM((PANEL, PANEL), jnp.float32),
            pltpu.VMEM((PANEL, 2 * PANEL), jnp.float32),
            pltpu.VMEM((16, 32, PANEL), jnp.float32),
            pltpu.VMEM((32, PANEL), jnp.float32),
            dma((NC, NZ)), dma((NC, NZ)), dma((NZ,)), dma((NZ,)),
            dma((2, NC, NZ)), dma((2, NC, NZ)), dma((NC, NZ)), dma((2, NC, NZ)),
            dma((NC, NP)), dma((NC, NP)), dma((NC, NP)), dma((2,)), dma((16,)), dma((2,)),
        ],
        compiler_params=pltpu.CompilerParams(
            collective_id=0, has_side_effects=True, vmem_limit_bytes=60 * 1024 * 1024),
    )(pair_dens, pair_index, val_energy, cond_energy, coul_root.reshape(64, 128))


def shards(pair_dens, pair_index, val_energy, cond_energy, coul_root):
    return tuple(epsilon_block(pair_dens, pair_index, val_energy, cond_energy, coul_root))


def solution(mesh):
    in_specs = (P("band", "comp"), P("band"), P(), P(), P())
    out_specs = (P("band", "comp"), P(("band", "comp"), None))
    return jax.shard_map(shards, mesh=mesh, in_specs=in_specs, out_specs=out_specs, check_vma=False)
```
